32 devices in a mesh: ut: 4 (over z), it: 8 (over y, x, core).
Axes of the slice: x: 2, y: 2, z: 4, core: 2. Of those that a mesh axis runs over, the one named last changes fastest.
Arguments:
- user_emb: float32 [2048, 512], P('ut'), may hold values from -1 to 1
- tag_emb: float32 [1024, 512], P('ut'), may hold values from -1 to 1
- item_emb: float32 [2048, 512], P('it'), may hold values from -1 to 1
- user_tile_block: int32 [128], P(('ut', 'it')), may hold values from 0 to 3
- user_tile_item: int32 [128], P(('ut', 'it')), may hold values from 0 to 1
- user_tile_counts: int32 [128, 128, 128], P(('ut', 'it')), may hold values from 0 to 3
- tag_tile_block: int32 [64], P(('ut', 'it')), may hold values from 0 to 1
- tag_tile_item: int32 [64], P(('ut', 'it')), may hold values from 0 to 1
- tag_tile_counts: int32 [64, 128, 128], P(('ut', 'it')), may hold values from 0 to 3
Outputs:
- item_block: float32 [2048, 128], P('it')
- user_block: float32 [2048, 128], P('ut')
- tag_block: float32 [1024, 128], P('ut')
The draws below stay inside these ranges and needn't reach their ends.
Inputs may be any that keep to these rules, and one draw needn't show every extreme that they name: `user_tile_block`: A pair of blocks may recur in several tiles of one device; their counts then add. `tag_tile_block`: A pair of blocks may recur in several tiles of one device; their counts then add.
All inputs are finite; a program needn't handle non-finite values.
Results may differ from the reference program's by a relative error of at most 0.0003.
Values sent between devices are 32-bit elements; how exact they have to be, the bound alone decides.
A program may use at most 64 MiB of HBM per device.

```python
import math
import jax
import jax.numpy as jnp
import numpy as np
from jax import lax

RANK = 512
BLK = 128
TILE = 128
CG_STEPS = 3
U_DEV = 512
TAG_DEV = 256
I_DEV = 256
UTILES = 4
TTILES = 2
USERS = 2048
TAGS = 1024
ITEMS = 2048
N_UT = 4
N_IT = 8


def with_ends(entries, rng, low, largest):
    extent = entries.shape
    spot = [jax.random.randint(jax.random.fold_in(rng, axis), (), 0, extent[axis]) for axis in range(len(extent))]
    entries = entries.at[tuple(spot)].set(low)
    longest = extent.index(max(extent))
    spot[longest] = (spot[longest] + 1) % extent[longest]
    return entries.at[tuple(spot)].set(largest)


def block_scale(stream_key, dims, shards, low, high):
    gain = 1.0
    for dim, blocks in shards:
        steps = jax.random.uniform(jax.random.fold_in(jax.random.fold_in(stream_key, 6), dim), (blocks,), jnp.float32, low / len(shards), high / len(shards))
        gain = gain * jnp.repeat(jnp.exp(steps), dims[dim] // blocks).reshape((-1,) + (1,) * (len(dims) - 1 - dim))
    return gain


def rank_table(amount, skew):
    portions = [(1 << 20) // math.isqrt(grade ** skew) + 1 for grade in range(1, amount + 1)]
    spread = 1 + sum(portions) // (1 << 30)
    return np.cumsum(np.array([max(1, weight // spread) for weight in portions]))


def ranked(stream_key, extent, number_of, lean):
    grid = rank_table(number_of, lean)
    lot = jax.random.randint(jax.random.fold_in(stream_key, 1), extent, 0, int(grid[number_of - 1]))
    grade = jnp.searchsorted(jnp.asarray(grid, jnp.int32), lot, side="right")
    return jax.random.permutation(jax.random.fold_in(stream_key, 2), number_of)[grade].astype(jnp.int32)


def centred(stream_key, dims, spread, reach, shards=(), held_as=jnp.bfloat16):
    factor_of = block_scale(stream_key, dims, shards, -0.22, 0.18) if shards else 1.0
    values = jax.random.normal(stream_key, dims, jnp.float32) * spread * factor_of
    return jnp.minimum(jnp.maximum(values, -reach), reach).astype(held_as)


def setup_inputs(seed: int = 0) -> dict:
    key_of = jax.random.split(jax.random.key(seed), 10)
    user_emb = centred(key_of[0], (USERS, RANK), 0.2, 1.0, ((0, 4),), jnp.float32)
    tag_emb = centred(key_of[1], (TAGS, RANK), 0.2, 1.0, ((0, 4),), jnp.float32)
    item_emb = centred(key_of[2], (ITEMS, RANK), 0.2, 1.0, ((0, 8),), jnp.float32)
    user_tile_block = with_ends(ranked(key_of[3], (N_UT * N_IT * UTILES,), U_DEV // TILE, 2), jax.random.fold_in(key_of[3], 3), 0, (U_DEV // TILE) - 1).astype(jnp.int32)
    user_tile_item = with_ends(jax.random.randint(key_of[4], (N_UT * N_IT * UTILES,), 0, I_DEV // TILE), jax.random.fold_in(key_of[4], 1), 0, (I_DEV // TILE) - 1).astype(jnp.int32)
    user_tile_counts = with_ends(jax.random.randint(key_of[5], (N_UT * N_IT * UTILES, TILE, TILE), 0, 4), jax.random.fold_in(key_of[5], 1), 0, 3).astype(jnp.int32)
    tag_tile_block = with_ends(ranked(key_of[6], (N_UT * N_IT * TTILES,), TAG_DEV // TILE, 2), jax.random.fold_in(key_of[6], 3), 0, (TAG_DEV // TILE) - 1).astype(jnp.int32)
    tag_tile_item = with_ends(jax.random.randint(key_of[7], (N_UT * N_IT * TTILES,), 0, I_DEV // TILE), jax.random.fold_in(key_of[7], 1), 0, (I_DEV // TILE) - 1).astype(jnp.int32)
    tag_tile_counts = with_ends(jax.random.randint(key_of[8], (N_UT * N_IT * TTILES, TILE, TILE), 0, 4), jax.random.fold_in(key_of[8], 1), 0, 3).astype(jnp.int32)
    return {"user_emb": user_emb, "tag_emb": tag_emb, "item_emb": item_emb, "user_tile_block": user_tile_block, "user_tile_item": user_tile_item, "user_tile_counts": user_tile_counts, "tag_tile_block": tag_tile_block, "tag_tile_item": tag_tile_item, "tag_tile_counts": tag_tile_counts}


CONFIDENCE = 0.5
UNSEEN_WEIGHT = 0.1
PENALTY = 1.0
EPSILON = 1e-6
EXACT_PRECISION = lax.Precision.HIGHEST


def pick_blocks(values, which, block_count):
    indicator_matrix = (which[:, None] == jnp.arange(block_count, dtype=jnp.int32)[None, :]).astype(jnp.float32)
    block_list = values.reshape(block_count, values.shape[0] // block_count, values.shape[1])
    return jnp.einsum("dq,qsp->dsp", indicator_matrix, block_list, precision=EXACT_PRECISION)


def insert_blocks(tile_collection, which, block_count):
    indicator_matrix = (which[:, None] == jnp.arange(block_count, dtype=jnp.int32)[None, :]).astype(jnp.float32)
    reduced_sum = jnp.einsum("jx,jsv->xsv", indicator_matrix, tile_collection, precision=EXACT_PRECISION)
    return reduced_sum.reshape(block_count * tile_collection.shape[1], tile_collection.shape[2])


def item_terms(row_tiles, item_tiles, weight, offset, item_which, item_count):
    predicted = jnp.einsum("trk,tik->tri", row_tiles, item_tiles, precision=EXACT_PRECISION)
    leftover = weight * (1.0 - predicted)
    row_cols = lax.dynamic_slice_in_dim(row_tiles, offset, BLK, 2)
    tile_terms = jnp.einsum("tri,trj->tij", leftover, row_cols, precision=EXACT_PRECISION)
    return insert_blocks(tile_terms, item_which, item_count)


def item_product(row_cols, weight, direction, item_which, item_count):
    picked = pick_blocks(direction, item_which, item_count)
    inner_sum = jnp.einsum("trj,tij->tri", row_cols, picked, precision=EXACT_PRECISION)
    tile_terms = jnp.einsum("tri,trj->tij", weight * inner_sum, row_cols, precision=EXACT_PRECISION)
    return insert_blocks(tile_terms, item_which, item_count)


def row_terms(row_tiles, item_tiles, weight, offset, row_which, row_count):
    predicted = jnp.einsum("trk,tik->tri", row_tiles, item_tiles, precision=EXACT_PRECISION)
    leftover = weight * (1.0 - predicted)
    item_cols = lax.dynamic_slice_in_dim(item_tiles, offset, BLK, 2)
    tile_terms = jnp.einsum("tri,tij->trj", leftover, item_cols, precision=EXACT_PRECISION)
    return insert_blocks(tile_terms, row_which, row_count)


def row_product(item_cols, weight, direction, row_which, row_count):
    picked = pick_blocks(direction, row_which, row_count)
    inner_sum = jnp.einsum("trj,tij->tri", picked, item_cols, precision=EXACT_PRECISION)
    tile_terms = jnp.einsum("tri,tij->trj", weight * inner_sum, item_cols, precision=EXACT_PRECISION)
    return insert_blocks(tile_terms, row_which, row_count)


def conjugate(right_side, operator_fn):
    result = jnp.zeros_like(right_side)
    leftover = right_side
    direction = right_side
    norm_now = jnp.sum(leftover * leftover, axis=1, keepdims=True)
    for iteration in range(CG_STEPS):
        applied = operator_fn(direction)
        step_length = norm_now / (jnp.sum(direction * applied, axis=1, keepdims=True) + EPSILON)
        result = result + step_length * direction
        leftover = leftover - step_length * applied
        norm_next = jnp.sum(leftover * leftover, axis=1, keepdims=True)
        direction = leftover + norm_next / (norm_now + EPSILON) * direction
        norm_now = norm_next
    return result


def reference(user_emb, tag_emb, item_emb, user_tile_block, user_tile_item, user_tile_counts, tag_tile_block, tag_tile_item, tag_tile_counts):
    offset = 0
    user_which = user_tile_block.reshape(N_UT, N_IT, UTILES)
    user_item = user_tile_item.reshape(N_UT, N_IT, UTILES)
    user_count = user_tile_counts.reshape(N_UT, N_IT, UTILES, TILE, TILE)
    tag_which = tag_tile_block.reshape(N_UT, N_IT, TTILES)
    tag_item = tag_tile_item.reshape(N_UT, N_IT, TTILES)
    tag_count = tag_tile_counts.reshape(N_UT, N_IT, TTILES, TILE, TILE)
    user_blocks = U_DEV // TILE
    tag_blocks = TAG_DEV // TILE
    item_blocks = I_DEV // TILE

    def extract_rows(values, shard_id, size):
        return lax.dynamic_slice_in_dim(values, (shard_id * size).astype(jnp.int32), size, 0)

    def shard_tiles(row_shard, col_shard, item_table):
        user_rows = extract_rows(user_emb, row_shard, U_DEV)
        tag_rows = extract_rows(tag_emb, row_shard, TAG_DEV)
        item_rows = extract_rows(item_table, col_shard, I_DEV)
        user_part = (pick_blocks(user_rows, user_which[row_shard, col_shard], user_blocks),
                     pick_blocks(item_rows, user_item[row_shard, col_shard], item_blocks),
                     CONFIDENCE * user_count[row_shard, col_shard].astype(jnp.float32),
                     user_which[row_shard, col_shard], user_item[row_shard, col_shard])
        tag_part = (pick_blocks(tag_rows, tag_which[row_shard, col_shard], tag_blocks),
                    pick_blocks(item_rows, tag_item[row_shard, col_shard], item_blocks),
                    CONFIDENCE * tag_count[row_shard, col_shard].astype(jnp.float32),
                    tag_which[row_shard, col_shard], tag_item[row_shard, col_shard])
        return user_part, tag_part

    def item_pass(tile_fn):
        def per_column(col_shard):
            def accumulate(row_shard, running):
                user_part, tag_part = shard_tiles(row_shard, col_shard, item_emb)
                return running + tile_fn(user_part, tag_part, col_shard)
            return lax.fori_loop(0, N_UT, accumulate, jnp.zeros((I_DEV, BLK), jnp.float32))
        return lax.map(per_column, jnp.arange(N_IT, dtype=jnp.int32)).reshape(ITEMS, BLK)

    def item_observed(user_part, tag_part, col_shard):
        return (item_terms(user_part[0], user_part[1], user_part[2], offset, user_part[4], item_blocks)
                + item_terms(tag_part[0], tag_part[1], tag_part[2], offset, tag_part[4], item_blocks))

    user_cols = lax.dynamic_slice_in_dim(user_emb, offset, BLK, 1)
    tag_cols = lax.dynamic_slice_in_dim(tag_emb, offset, BLK, 1)
    item_cols = lax.dynamic_slice_in_dim(item_emb, offset, BLK, 1)
    gram_rows = (jnp.einsum("rj,rk->jk", user_cols, user_emb, precision=EXACT_PRECISION)
                 + jnp.einsum("rj,rk->jk", tag_cols, tag_emb, precision=EXACT_PRECISION))
    gram_square = lax.dynamic_slice_in_dim(gram_rows, offset, BLK, 1)
    item_right = (item_pass(item_observed)
                  - UNSEEN_WEIGHT * jnp.einsum("ik,jk->ij", item_emb, gram_rows, precision=EXACT_PRECISION)
                  - PENALTY * item_cols)

    def item_operator(direction):
        def tile_fn(user_part, tag_part, col_shard):
            local_dir = extract_rows(direction, col_shard, I_DEV)
            return (item_product(lax.dynamic_slice_in_dim(user_part[0], offset, BLK, 2), user_part[2], local_dir, user_part[4], item_blocks)
                    + item_product(lax.dynamic_slice_in_dim(tag_part[0], offset, BLK, 2), tag_part[2], local_dir, tag_part[4], item_blocks))
        return (item_pass(tile_fn)
                + UNSEEN_WEIGHT * jnp.dot(direction, gram_square, precision=EXACT_PRECISION, preferred_element_type=jnp.float32)
                + PENALTY * direction)

    item_block = item_cols + conjugate(item_right, item_operator)
    new_items = lax.dynamic_update_slice_in_dim(item_emb, item_block, offset, 1)

    def row_pass(tile_fn):
        def per_row(row_shard):
            def accumulate(col_shard, running):
                user_part, tag_part = shard_tiles(row_shard, col_shard, new_items)
                addition = tile_fn(user_part, tag_part, row_shard)
                return (running[0] + addition[0], running[1] + addition[1])
            start_value = (jnp.zeros((U_DEV, BLK), jnp.float32), jnp.zeros((TAG_DEV, BLK), jnp.float32))
            return lax.fori_loop(0, N_IT, accumulate, start_value)
        user_sum, tag_sum = lax.map(per_row, jnp.arange(N_UT, dtype=jnp.int32))
        return jnp.concatenate([user_sum.reshape(USERS, BLK), tag_sum.reshape(TAGS, BLK)], axis=0)

    def row_observed(user_part, tag_part, row_shard):
        return (row_terms(user_part[0], user_part[1], user_part[2], offset, user_part[3], user_blocks),
                row_terms(tag_part[0], tag_part[1], tag_part[2], offset, tag_part[3], tag_blocks))

    item_gram = jnp.einsum("ij,ik->jk", item_block, new_items, precision=EXACT_PRECISION)
    item_square = lax.dynamic_slice_in_dim(item_gram, offset, BLK, 1)
    all_rows = jnp.concatenate([user_emb, tag_emb], axis=0)
    row_cols = jnp.concatenate([user_cols, tag_cols], axis=0)
    row_right = (row_pass(row_observed)
                 - UNSEEN_WEIGHT * jnp.einsum("rk,jk->rj", all_rows, item_gram, precision=EXACT_PRECISION)
                 - PENALTY * row_cols)

    def row_operator(direction):
        def tile_fn(user_part, tag_part, row_shard):
            user_dir = extract_rows(direction[:USERS], row_shard, U_DEV)
            tag_dir = extract_rows(direction[USERS:], row_shard, TAG_DEV)
            return (row_product(lax.dynamic_slice_in_dim(user_part[1], offset, BLK, 2), user_part[2], user_dir, user_part[3], user_blocks),
                    row_product(lax.dynamic_slice_in_dim(tag_part[1], offset, BLK, 2), tag_part[2], tag_dir, tag_part[3], tag_blocks))
        return (row_pass(tile_fn)
                + UNSEEN_WEIGHT * jnp.dot(direction, item_square, precision=EXACT_PRECISION, preferred_element_type=jnp.float32)
                + PENALTY * direction)

    solution = row_cols + conjugate(row_right, row_operator)
    return item_block, solution[:USERS], solution[USERS:]
```

```python
import functools

import jax
import jax.numpy as jnp
from jax import lax
from jax.experimental import pallas as pl
from jax.experimental.pallas import tpu as pltpu
from jax.sharding import PartitionSpec as P

BLK = 128
CG_STEPS = 3


CONFIDENCE = 0.5
UNSEEN_WEIGHT = 0.1
PENALTY = 1.0
EPSILON = 1e-06
EXACT_PRECISION = lax.Precision.HIGHEST


def pick_blocks(values, which, block_count):
    indicator_matrix = (which[:, None] == jnp.arange(block_count, dtype=jnp.int32)[None, :]).astype(
        jnp.float32
    )
    block_list = values.reshape(block_count, values.shape[0] // block_count, values.shape[1])
    return jnp.einsum("dq,qsp->dsp", indicator_matrix, block_list, precision=EXACT_PRECISION)


def insert_blocks(tile_collection, which, block_count):
    indicator_matrix = (which[:, None] == jnp.arange(block_count, dtype=jnp.int32)[None, :]).astype(
        jnp.float32
    )
    reduced_sum = jnp.einsum(
        "jx,jsv->xsv", indicator_matrix, tile_collection, precision=EXACT_PRECISION
    )
    return reduced_sum.reshape(block_count * tile_collection.shape[1], tile_collection.shape[2])


def item_terms(row_tiles, item_tiles, weight, offset, item_which, item_count):
    predicted = jnp.einsum("trk,tik->tri", row_tiles, item_tiles, precision=EXACT_PRECISION)
    leftover = weight * (1.0 - predicted)
    row_cols = lax.dynamic_slice_in_dim(row_tiles, offset, BLK, 2)
    tile_terms = jnp.einsum("tri,trj->tij", leftover, row_cols, precision=EXACT_PRECISION)
    return insert_blocks(tile_terms, item_which, item_count)


def item_product(row_cols, weight, direction, item_which, item_count):
    picked = pick_blocks(direction, item_which, item_count)
    inner_sum = jnp.einsum("trj,tij->tri", row_cols, picked, precision=EXACT_PRECISION)
    tile_terms = jnp.einsum("tri,trj->tij", weight * inner_sum, row_cols, precision=EXACT_PRECISION)
    return insert_blocks(tile_terms, item_which, item_count)


def row_terms(row_tiles, item_tiles, weight, offset, row_which, row_count):
    predicted = jnp.einsum("trk,tik->tri", row_tiles, item_tiles, precision=EXACT_PRECISION)
    leftover = weight * (1.0 - predicted)
    item_cols = lax.dynamic_slice_in_dim(item_tiles, offset, BLK, 2)
    tile_terms = jnp.einsum("tri,tij->trj", leftover, item_cols, precision=EXACT_PRECISION)
    return insert_blocks(tile_terms, row_which, row_count)


def row_product(item_cols, weight, direction, row_which, row_count):
    picked = pick_blocks(direction, row_which, row_count)
    inner_sum = jnp.einsum("trj,tij->tri", picked, item_cols, precision=EXACT_PRECISION)
    tile_terms = jnp.einsum(
        "tri,tij->trj", weight * inner_sum, item_cols, precision=EXACT_PRECISION
    )
    return insert_blocks(tile_terms, row_which, row_count)


def conjugate(right_side, operator_fn):
    result = jnp.zeros_like(right_side)
    leftover = right_side
    direction = right_side
    norm_now = jnp.sum(leftover * leftover, axis=1, keepdims=True)
    for iteration in range(CG_STEPS):
        applied = operator_fn(direction)
        step_length = norm_now / (jnp.sum(direction * applied, axis=1, keepdims=True) + EPSILON)
        result = result + step_length * direction
        leftover = leftover - step_length * applied
        norm_next = jnp.sum(leftover * leftover, axis=1, keepdims=True)
        direction = leftover + norm_next / (norm_now + EPSILON) * direction
        norm_now = norm_next
    return result


def local(
    user_emb,
    tag_emb,
    item_emb,
    user_tile_block,
    user_tile_item,
    user_tile_counts,
    tag_tile_block,
    tag_tile_item,
    tag_tile_counts,
):
    tile_size = user_tile_counts.shape[1]
    user_blocks = user_emb.shape[0] // tile_size
    tag_blocks = tag_emb.shape[0] // tile_size
    item_blocks = item_emb.shape[0] // tile_size
    user_total = user_emb.shape[0]
    offset = 0
    user_weight = CONFIDENCE * user_tile_counts.astype(jnp.float32)
    tag_weight = CONFIDENCE * tag_tile_counts.astype(jnp.float32)
    user_tiles = pick_blocks(user_emb, user_tile_block, user_blocks)
    tag_tiles = pick_blocks(tag_emb, tag_tile_block, tag_blocks)
    user_col_tiles = lax.dynamic_slice_in_dim(user_tiles, offset, BLK, 2)
    tag_col_tiles = lax.dynamic_slice_in_dim(tag_tiles, offset, BLK, 2)
    items_for_users = pick_blocks(item_emb, user_tile_item, item_blocks)
    items_for_tags = pick_blocks(item_emb, tag_tile_item, item_blocks)
    user_cols = lax.dynamic_slice_in_dim(user_emb, offset, BLK, 1)
    tag_cols = lax.dynamic_slice_in_dim(tag_emb, offset, BLK, 1)
    item_cols = lax.dynamic_slice_in_dim(item_emb, offset, BLK, 1)
    gram_part = jnp.einsum(
        "rj,rk->jk", user_cols, user_emb, precision=EXACT_PRECISION
    ) + jnp.einsum("rj,rk->jk", tag_cols, tag_emb, precision=EXACT_PRECISION)
    observed_part = item_terms(
        user_tiles, items_for_users, user_weight, offset, user_tile_item, item_blocks
    ) + item_terms(tag_tiles, items_for_tags, tag_weight, offset, tag_tile_item, item_blocks)
    gram_rows, observed = lax.psum((gram_part, observed_part), "ut")
    gram_square = lax.dynamic_slice_in_dim(gram_rows, offset, BLK, 1)
    item_right = (
        observed
        - UNSEEN_WEIGHT * jnp.einsum("ik,jk->ij", item_emb, gram_rows, precision=EXACT_PRECISION)
        - PENALTY * item_cols
    )

    def item_operator(direction):
        local_part = item_product(
            user_col_tiles, user_weight, direction, user_tile_item, item_blocks
        ) + item_product(tag_col_tiles, tag_weight, direction, tag_tile_item, item_blocks)
        return (
            lax.psum(local_part, "ut")
            + UNSEEN_WEIGHT
            * jnp.dot(
                direction,
                gram_square,
                precision=EXACT_PRECISION,
                preferred_element_type=jnp.float32,
            )
            + PENALTY * direction
        )

    item_block = item_cols + conjugate(item_right, item_operator)
    new_items = lax.dynamic_update_slice_in_dim(item_emb, item_block, offset, 1)
    new_for_users = pick_blocks(new_items, user_tile_item, item_blocks)
    new_for_tags = pick_blocks(new_items, tag_tile_item, item_blocks)
    user_item_cols = lax.dynamic_slice_in_dim(new_for_users, offset, BLK, 2)
    tag_item_cols = lax.dynamic_slice_in_dim(new_for_tags, offset, BLK, 2)
    gram_part_rows = jnp.einsum("ij,ik->jk", item_block, new_items, precision=EXACT_PRECISION)
    observed_rows = jnp.concatenate(
        [
            row_terms(user_tiles, new_for_users, user_weight, offset, user_tile_block, user_blocks),
            row_terms(tag_tiles, new_for_tags, tag_weight, offset, tag_tile_block, tag_blocks),
        ],
        axis=0,
    )
    all_rows = jnp.concatenate([user_emb, tag_emb], axis=0)
    row_cols = jnp.concatenate([user_cols, tag_cols], axis=0)

    def row_local(direction):
        return jnp.concatenate(
            [
                row_product(
                    user_item_cols,
                    user_weight,
                    direction[:user_total],
                    user_tile_block,
                    user_blocks,
                ),
                row_product(
                    tag_item_cols, tag_weight, direction[user_total:], tag_tile_block, tag_blocks
                ),
            ],
            axis=0,
        )

    item_gram, observed_sum = lax.psum((gram_part_rows, observed_rows), "it")
    item_square = lax.dynamic_slice_in_dim(item_gram, offset, BLK, 1)
    row_right = (
        observed_sum
        - UNSEEN_WEIGHT * jnp.einsum("rk,jk->rj", all_rows, item_gram, precision=EXACT_PRECISION)
        - PENALTY * row_cols
    )

    def row_operator(direction):
        return (
            lax.psum(row_local(direction), "it")
            + UNSEEN_WEIGHT
            * jnp.dot(
                direction,
                item_square,
                precision=EXACT_PRECISION,
                preferred_element_type=jnp.float32,
            )
            + PENALTY * direction
        )

    solution = row_cols + conjugate(row_right, row_operator)
    return (item_block, solution[:user_total], solution[user_total:])


BF16 = jnp.bfloat16
F32 = jnp.float32
MESH = pl.DeviceIdType.MESH


def halves(value):
    high = value.astype(BF16)
    return high, (value - high.astype(F32)).astype(BF16)


def dot_nt(left, right):
    return lax.dot_general(left, right, (((1,), (1,)), ((), ())), preferred_element_type=F32)


def dot_nn(left, right):
    return lax.dot_general(left, right, (((1,), (0,)), ((), ())), preferred_element_type=F32)


def stacked(value):
    return jnp.concatenate(halves(value), axis=0)


def paired(value):
    return jnp.concatenate(halves(value), axis=1)


def twice(value):
    both = stacked(value)
    return jnp.concatenate([both, both], axis=1)


def fold(total):
    rows = total.shape[0] // 2
    return total[:rows, :BLK] + total[:rows, BLK:] + total[rows:, :BLK] + total[rows:, BLK:]


def fold_rows(total):
    rows = total.shape[0] // 2
    return total[:rows] + total[rows:]


def solve(right_side, weight_ref, table_ref):
    chunks = weight_ref.shape[0]

    def step(_, carry):
        result, leftover, direction, norm_now = carry
        operand = twice(direction)
        total = None
        for j in range(chunks):
            inner = fold_rows(dot_nt(operand, table_ref[j]))
            term = dot_nn(stacked(weight_ref[j] * inner), table_ref[j])
            total = term if total is None else total + term
        applied = fold(total) + PENALTY * direction
        length = norm_now / (jnp.sum(direction * applied, axis=1, keepdims=True) + EPSILON)
        result = result + length * direction
        leftover = leftover - length * applied
        norm_next = jnp.sum(leftover * leftover, axis=1, keepdims=True)
        direction = leftover + norm_next / (norm_now + EPSILON) * direction
        return result, leftover, direction, norm_next

    norm = jnp.sum(right_side * right_side, axis=1, keepdims=True)
    start = (jnp.zeros_like(right_side), right_side, right_side, norm)
    return lax.fori_loop(0, CG_STEPS, step, start)[0]


def kernel(
    nu, ni, total_copies,
    ub_ref, ui_ref, tb_ref, ti_ref,
    user_ref, tag_ref, item_ref, uc_ref, tc_ref,
    item_out, user_out, tag_out,
    place, place_u, place_i, at, rat, ar, rar, wj, w2, hh, hl, e0, re0, est, part, rpart,
    at_own, a_own, ib, ib2, out, send_sem, recv_sem,
):
    k = lax.axis_index("ut")
    m = lax.axis_index("it")
    tile = uc_ref.shape[1]
    ut, tt = uc_ref.shape[0], tc_ref.shape[0]
    users, tags, items = user_ref.shape[0], tag_ref.shape[0], item_ref.shape[0]
    nub, ntb, nib = users // tile, tags // tile, items // tile
    nrb = nub + ntb
    rows = users + tags
    sub_i, sub_r = tile // nu, tile // ni
    share = rows // ni
    chips = ni // 2
    chip, core = m // 2, m % 2
    other = 1 - core
    sibling = 2 * chip + other

    def u_to(d):
        return (k + d) % nu

    def u_from(d):
        return (k + nu - d) % nu

    def i_to(d):
        return (m + d) % ni

    def i_from(d):
        return (m + ni - d) % ni

    def c_to(d):
        return (chip + d) % chips

    def c_from(d):
        return (chip + chips - d) % chips

    sent = []
    count = [0]

    def ticket():
        count[0] += 1
        return count[0] - 1

    def copy(number, source, target, device):
        return pltpu.make_async_remote_copy(
            src_ref=source, dst_ref=target, send_sem=send_sem.at[number],
            recv_sem=recv_sem.at[number], device_id=device, device_id_type=MESH,
        )

    def send(number, source, target, device):
        moving = copy(number, source, target, device)
        moving.start()
        sent.append(moving)

    def arrived(number, target):
        copy(number, target, target, (u_to(1), m)).wait_recv()

    barrier = pltpu.get_barrier_semaphore()
    for d in range(1, nu):
        pl.semaphore_signal(barrier, inc=1, device_id=(u_to(d), m), device_id_type=MESH)
    for d in range(1, ni):
        pl.semaphore_signal(barrier, inc=1, device_id=(k, i_to(d)), device_id_type=MESH)

    wj[k, 0:users, :] = user_ref[:, 0:BLK]
    wj[k, users:rows, :] = tag_ref[:, 0:BLK]
    line = lax.broadcasted_iota(jnp.int32, place.shape, 0)
    spots = jnp.zeros(place.shape, jnp.int32)
    for t in range(ut):
        spots = jnp.where(line == t, ub_ref[t] * nib + ui_ref[t], spots)
    for t in range(tt):
        spots = jnp.where(line == ut + t, (nub + tb_ref[t]) * nib + ti_ref[t], spots)
    place[...] = spots
    for t in range(ut + tt):
        counts = CONFIDENCE * (uc_ref[t] if t < ut else tc_ref[t - ut]).astype(F32)
        ar[t] = counts
        at[t] = counts.T

    pl.semaphore_wait(barrier, nu + ni - 2)

    def w_slice(kk, mm):
        return wj.at[kk, pl.ds(pl.multiple_of(mm * share, 8), share), :]

    def b_slice(kk, mm):
        return ib.at[mm, :, pl.ds(pl.multiple_of(kk * sub_i, 8), sub_i), :]

    far = sorted(range(1, nu), key=lambda d: min(d, nu - d))

    def tickets(first):
        z = {d: ticket() for d in range(1, nu)}
        p = {(d, e): ticket() for d in range(first, nu) for e in range(1, chips)}
        s = {(d, e): ticket() for d in range(first, nu) for e in range(chips)}
        return z, p, s

    def spread_along(piece, marks):
        for d in far:
            send(marks[0][d], piece(k, m), piece(k, m), (u_to(d), m))

    def spread_plane(piece, marks, d):
        held = piece(u_from(d), m)
        for e in range(1, chips):
            send(marks[1][d, e], held, held, (k, 2 * c_to(e) + core))
        send(marks[2][d, 0], held, held, (k, sibling))

    def spread_sibling(piece, marks, d):
        for e in range(1, chips):
            held = piece(u_from(d), 2 * c_from(e) + core)
            arrived(marks[1][d, e], held)
            send(marks[2][d, e], held, held, (k, sibling))

    def spread_finish(piece, marks, d):
        for e in range(chips):
            arrived(marks[2][d, e], piece(u_from(d), 2 * c_from(e) + other))

    w_marks = tickets(1)
    spread_along(w_slice, w_marks)
    at_marks = {d: (ticket(), ticket()) for d in range(1, nu)}

    def at_cut(kk):
        return at.at[:, pl.ds(pl.multiple_of(kk * sub_i, 8), sub_i), :]

    def r_cut(ref, mm):
        return ref.at[:, pl.ds(pl.multiple_of(mm * sub_r, 8), sub_r), :]

    for d in far:
        send(at_marks[d][0], at_cut(u_to(d)), rat.at[k], (u_to(d), m))
        send(at_marks[d][1], place, place_u.at[k], (u_to(d), m))
    ar_marks = {d: (ticket(), ticket()) for d in range(1, ni)}
    for d in range(1, ni):
        send(ar_marks[d][0], r_cut(ar, i_to(d)), rar.at[m], (k, i_to(d)))
        send(ar_marks[d][1], place, place_i.at[m], (k, i_to(d)))
    rat[k] = at[:, pl.ds(pl.multiple_of(k * sub_i, 8), sub_i), :]
    rar[m] = ar[:, pl.ds(pl.multiple_of(m * sub_r, 8), sub_r), :]
    place_u[k] = place[...]
    place_i[m] = place[...]

    def dense(spot_rows, tiles, block, piece):
        total = None
        for t in (range(ut) if block < nub else range(ut, ut + tt)):
            code = block * nib + piece
            term = jnp.where(spot_rows[t : t + 1, :] == code, tiles(t), 0.0)
            total = term if total is None else total + term
        return total

    high, low = halves(item_ref[...])
    hh[...] = high
    hl[...] = low
    spot_rows = place[...]
    step = 2 if nub % 2 == 0 and ntb % 2 == 0 else 1

    def terms(first):
        block = user_ref[first * tile : (first + step) * tile, :] if first < nub else (
            tag_ref[(first - nub) * tile : (first - nub + step) * tile, :])
        rh, rl = halves(block)

        def product(cols):
            return (dot_nt(rh[:, cols], hh[:, cols]) + dot_nt(rh[:, cols], hl[:, cols])
                    + dot_nt(rl[:, cols], hh[:, cols]))

        rest = product(slice(BLK, None))
        mine = product(slice(0, BLK))
        counts = jnp.concatenate([
            jnp.concatenate([dense(spot_rows, lambda t: ar[t], b, p) for p in range(nib)], axis=1)
            for b in range(first, first + step)], axis=0)
        weight = counts + UNSEEN_WEIGHT
        begun = counts - weight * rest
        leftover = (begun - weight * mine).T
        eh, el = halves(leftover)
        span = slice(first * tile, (first + step) * tile)
        est[0:items, span] = eh
        est[items:, span] = el
        for b in range(step):
            e0[first + b] = begun[b * tile : (b + 1) * tile]

    firsts = list(range(0, nrb, step))
    for first in firsts[: len(firsts) // 2]:
        terms(first)
    for d in far:
        arrived(w_marks[0][d], w_slice(u_from(d), m))
        spread_plane(w_slice, w_marks, d)
    for first in firsts[len(firsts) // 2 :]:
        terms(first)
    w2[k] = paired(wj[k])
    summed = fold(dot_nn(est[...], w2[k]))
    for p in range(nib):
        part[p] = summed[p * tile : (p + 1) * tile]
    p_marks = {d: ticket() for d in range(1, nu)}
    for d in far:
        send(p_marks[d], at_like(part, u_to(d), sub_i), rpart.at[k], (u_to(d), m))
    rpart[k] = part[:, pl.ds(pl.multiple_of(k * sub_i, 8), sub_i), :]
    for d in far:
        spread_sibling(w_slice, w_marks, d)
    e_marks = {d: ticket() for d in range(1, ni)}
    for d in range(1, ni):
        send(e_marks[d], r_cut(e0, i_to(d)), re0.at[m], (k, i_to(d)))
    re0[m] = e0[:, pl.ds(pl.multiple_of(m * sub_r, 8), sub_r), :]

    for d in far:
        arrived(at_marks[d][0], rat.at[u_from(d)])
        arrived(at_marks[d][1], place_u.at[u_from(d)])

    def lay_items(kk, none):
        spot = place_u[kk]
        for p in range(nib):
            for b in range(nrb):
                at_own[kk, p * sub_i : (p + 1) * sub_i, b * tile : (b + 1) * tile] = (
                    dense(spot, lambda t: rat[kk, t], b, p) + UNSEEN_WEIGHT)
        return none

    lax.fori_loop(0, nu, lay_items, 0)
    for d in far:
        spread_finish(w_slice, w_marks, d)
        source = u_from(d)
        w2[source] = paired(wj[source])
    for d in far:
        arrived(p_marks[d], rpart.at[u_from(d)])
    observed = rpart[0]
    for kk in range(1, nu):
        observed = observed + rpart[kk]
    own_items = jnp.concatenate([
        item_ref[pl.ds(pl.multiple_of(p * tile + k * sub_i, 8), sub_i), 0:BLK] for p in range(nib)], axis=0)
    right = observed.reshape(nib * sub_i, BLK) - PENALTY * own_items
    block = own_items + solve(right, at_own, w2)
    ib[m, :, pl.ds(pl.multiple_of(k * sub_i, 8), sub_i), :] = block.reshape(nib, sub_i, BLK)

    b_marks = tickets(0)
    spread_along(b_slice, b_marks)
    spread_plane(b_slice, b_marks, 0)
    for d in range(1, ni):
        arrived(ar_marks[d][0], rar.at[i_from(d)])
        arrived(ar_marks[d][1], place_i.at[i_from(d)])

    for d in far:
        arrived(b_marks[0][d], b_slice(u_from(d), m))
        spread_plane(b_slice, b_marks, d)

    def lay_rows(mm, none):
        spot = place_i[mm]
        for b in range(nrb):
            for p in range(nib):
                a_own[mm, b * sub_r : (b + 1) * sub_r, p * tile : (p + 1) * tile] = (
                    dense(spot, lambda t: rar[mm, t], b, p) + UNSEEN_WEIGHT)
        return none

    lax.fori_loop(0, ni, lay_rows, 0)
    for d in [0] + far:
        spread_sibling(b_slice, b_marks, d)
    for d in range(1, ni):
        arrived(e_marks[d], re0.at[i_from(d)])
    own_rows = jnp.concatenate(
        [user_ref[pl.ds(pl.multiple_of(b * tile + m * sub_r, 8), sub_r), 0:BLK] for b in range(nub)]
        + [tag_ref[pl.ds(pl.multiple_of(b * tile + m * sub_r, 8), sub_r), 0:BLK] for b in range(ntb)], axis=0)
    operand = twice(own_rows)
    for d in [0] + far:
        spread_finish(b_slice, b_marks, d)

    def gather(mm, total):
        table = paired(ib[mm].reshape(items, BLK))
        ib2[mm] = table
        inner = fold_rows(dot_nt(operand, table))
        leftover = re0[mm].reshape(share, items) - a_own[mm] * inner
        return total + dot_nn(stacked(leftover), table)

    total = lax.fori_loop(0, ni, gather, jnp.zeros((2 * share, 2 * BLK), F32))
    right = fold(total) - PENALTY * own_rows
    final = own_rows + solve(right, a_own, ib2)
    out[:, pl.ds(pl.multiple_of(m * sub_r, 8), sub_r), :] = final.reshape(nrb, sub_r, BLK)
    o_marks = {d: ticket() for d in range(1, ni)}
    for d in range(1, ni):
        send(o_marks[d], r_cut(out, m), r_cut(out, m), (k, i_to(d)))
    item_out[...] = ib[m].reshape(items, BLK)
    for d in range(1, ni):
        arrived(o_marks[d], r_cut(out, i_from(d)))
    for b in range(nub):
        user_out[b * tile : (b + 1) * tile, :] = out[b]
    for b in range(ntb):
        tag_out[b * tile : (b + 1) * tile, :] = out[nub + b]
    for moving in sent:
        moving.wait_send()
    if count[0] != total_copies:
        raise ValueError(count[0])


def at_like(ref, index, size):
    return ref.at[:, pl.ds(pl.multiple_of(index * size, 8), size), :]


def fused(
    nu, ni, user_emb, tag_emb, item_emb, user_tile_block, user_tile_item, user_tile_counts,
    tag_tile_block, tag_tile_item, tag_tile_counts,
):
    tile = user_tile_counts.shape[1]
    tiles = user_tile_counts.shape[0] + tag_tile_counts.shape[0]
    users, tags, (items, rank) = user_emb.shape[0], tag_emb.shape[0], item_emb.shape
    rows = users + tags
    nrb, nib = rows // tile, items // tile
    sub_i, sub_r, share, chips = tile // nu, tile // ni, rows // ni, ni // 2
    lines = -(-tiles // 8) * 8
    copies = (
        (nu - 1) + (nu - 1) * (2 * chips - 1) + (nu - 1) + nu * (2 * chips - 1)
        + 3 * (nu - 1) + 4 * (ni - 1)
    )
    vmem = pl.BlockSpec(memory_space=pltpu.VMEM)
    smem = pl.BlockSpec(memory_space=pltpu.SMEM)
    return pl.pallas_call(
        functools.partial(kernel, nu, ni, copies),
        out_shape=(
            jax.ShapeDtypeStruct((items, BLK), F32),
            jax.ShapeDtypeStruct((users, BLK), F32),
            jax.ShapeDtypeStruct((tags, BLK), F32),
        ),
        in_specs=[smem] * 4 + [vmem] * 5,
        out_specs=(vmem, vmem, vmem),
        scratch_shapes=[
            pltpu.VMEM((lines, 128), jnp.int32),
            pltpu.VMEM((nu, lines, 128), jnp.int32),
            pltpu.VMEM((ni, lines, 128), jnp.int32),
            pltpu.VMEM((tiles, tile, tile), F32),
            pltpu.VMEM((nu, tiles, sub_i, tile), F32),
            pltpu.VMEM((tiles, tile, tile), F32),
            pltpu.VMEM((ni, tiles, sub_r, tile), F32),
            pltpu.VMEM((nu, rows, BLK), F32),
            pltpu.VMEM((nu, rows, 2 * BLK), BF16),
            pltpu.VMEM((items, rank), BF16),
            pltpu.VMEM((items, rank), BF16),
            pltpu.VMEM((nrb, tile, items), F32),
            pltpu.VMEM((ni, nrb, sub_r, items), F32),
            pltpu.VMEM((2 * items, rows), BF16),
            pltpu.VMEM((nib, tile, BLK), F32),
            pltpu.VMEM((nu, nib, sub_i, BLK), F32),
            pltpu.VMEM((nu, nib * sub_i, rows), F32),
            pltpu.VMEM((ni, share, items), F32),
            pltpu.VMEM((ni, nib, tile, BLK), F32),
            pltpu.VMEM((ni, items, 2 * BLK), BF16),
            pltpu.VMEM((nrb, tile, BLK), F32),
            pltpu.SemaphoreType.DMA((copies,)),
            pltpu.SemaphoreType.DMA((copies,)),
        ],
        compiler_params=pltpu.CompilerParams(
            collective_id=0, has_side_effects=True, vmem_limit_bytes=48 * 1024 * 1024
        ),
    )(
        user_tile_block, user_tile_item, tag_tile_block, tag_tile_item,
        user_emb, tag_emb, item_emb, user_tile_counts, tag_tile_counts,
    )


def serves(nu, ni, tile):
    return nu > 1 and ni > 2 and ni % 2 == 0 and tile % (nu * 8) == 0 and tile % (ni * 16) == 0


def solution(mesh):
    placed = (
        P("ut", None),
        P("ut", None),
        P("it", None),
        P(("ut", "it")),
        P(("ut", "it")),
        P(("ut", "it"), None, None),
        P(("ut", "it")),
        P(("ut", "it")),
        P(("ut", "it"), None, None),
    )
    nu, ni = mesh.shape["ut"], mesh.shape["it"]

    def run(*arrays):
        if serves(nu, ni, arrays[5].shape[1]):
            return fused(nu, ni, *arrays)
        return local(*arrays)

    return jax.shard_map(
        run,
        mesh=mesh,
        in_specs=placed,
        out_specs=(P("it", None), P("ut", None), P("ut", None)),
        check_vma=False,
    )
```

```python
import functools

import jax
import jax.numpy as jnp
from jax import lax
from jax.experimental import pallas as pl
from jax.experimental.pallas import tpu as pltpu
from jax.sharding import PartitionSpec as P

BLK = 128
CG_STEPS = 3


CONFIDENCE = 0.5
UNSEEN_WEIGHT = 0.1
PENALTY = 1.0
EPSILON = 1e-06
EXACT_PRECISION = lax.Precision.HIGHEST


def pick_blocks(values, which, block_count):
    indicator_matrix = (which[:, None] == jnp.arange(block_count, dtype=jnp.int32)[None, :]).astype(
        jnp.float32
    )
    block_list = values.reshape(block_count, values.shape[0] // block_count, values.shape[1])
    return jnp.einsum("dq,qsp->dsp", indicator_matrix, block_list, precision=EXACT_PRECISION)


def insert_blocks(tile_collection, which, block_count):
    indicator_matrix = (which[:, None] == jnp.arange(block_count, dtype=jnp.int32)[None, :]).astype(
        jnp.float32
    )
    reduced_sum = jnp.einsum(
        "jx,jsv->xsv", indicator_matrix, tile_collection, precision=EXACT_PRECISION
    )
    return reduced_sum.reshape(block_count * tile_collection.shape[1], tile_collection.shape[2])


def item_terms(row_tiles, item_tiles, weight, offset, item_which, item_count):
    predicted = jnp.einsum("trk,tik->tri", row_tiles, item_tiles, precision=EXACT_PRECISION)
    leftover = weight * (1.0 - predicted)
    row_cols = lax.dynamic_slice_in_dim(row_tiles, offset, BLK, 2)
    tile_terms = jnp.einsum("tri,trj->tij", leftover, row_cols, precision=EXACT_PRECISION)
    return insert_blocks(tile_terms, item_which, item_count)


def item_product(row_cols, weight, direction, item_which, item_count):
    picked = pick_blocks(direction, item_which, item_count)
    inner_sum = jnp.einsum("trj,tij->tri", row_cols, picked, precision=EXACT_PRECISION)
    tile_terms = jnp.einsum("tri,trj->tij", weight * inner_sum, row_cols, precision=EXACT_PRECISION)
    return insert_blocks(tile_terms, item_which, item_count)


def row_terms(row_tiles, item_tiles, weight, offset, row_which, row_count):
    predicted = jnp.einsum("trk,tik->tri", row_tiles, item_tiles, precision=EXACT_PRECISION)
    leftover = weight * (1.0 - predicted)
    item_cols = lax.dynamic_slice_in_dim(item_tiles, offset, BLK, 2)
    tile_terms = jnp.einsum("tri,tij->trj", leftover, item_cols, precision=EXACT_PRECISION)
    return insert_blocks(tile_terms, row_which, row_count)


def row_product(item_cols, weight, direction, row_which, row_count):
    picked = pick_blocks(direction, row_which, row_count)
    inner_sum = jnp.einsum("trj,tij->tri", picked, item_cols, precision=EXACT_PRECISION)
    tile_terms = jnp.einsum(
        "tri,tij->trj", weight * inner_sum, item_cols, precision=EXACT_PRECISION
    )
    return insert_blocks(tile_terms, row_which, row_count)


def conjugate(right_side, operator_fn):
    result = jnp.zeros_like(right_side)
    leftover = right_side
    direction = right_side
    norm_now = jnp.sum(leftover * leftover, axis=1, keepdims=True)
    for iteration in range(CG_STEPS):
        applied = operator_fn(direction)
        step_length = norm_now / (jnp.sum(direction * applied, axis=1, keepdims=True) + EPSILON)
        result = result + step_length * direction
        leftover = leftover - step_length * applied
        norm_next = jnp.sum(leftover * leftover, axis=1, keepdims=True)
        direction = leftover + norm_next / (norm_now + EPSILON) * direction
        norm_now = norm_next
    return result


def local(
    user_emb,
    tag_emb,
    item_emb,
    user_tile_block,
    user_tile_item,
    user_tile_counts,
    tag_tile_block,
    tag_tile_item,
    tag_tile_counts,
):
    tile_size = user_tile_counts.shape[1]
    user_blocks = user_emb.shape[0] // tile_size
    tag_blocks = tag_emb.shape[0] // tile_size
    item_blocks = item_emb.shape[0] // tile_size
    user_total = user_emb.shape[0]
    offset = 0
    user_weight = CONFIDENCE * user_tile_counts.astype(jnp.float32)
    tag_weight = CONFIDENCE * tag_tile_counts.astype(jnp.float32)
    user_tiles = pick_blocks(user_emb, user_tile_block, user_blocks)
    tag_tiles = pick_blocks(tag_emb, tag_tile_block, tag_blocks)
    user_col_tiles = lax.dynamic_slice_in_dim(user_tiles, offset, BLK, 2)
    tag_col_tiles = lax.dynamic_slice_in_dim(tag_tiles, offset, BLK, 2)
    items_for_users = pick_blocks(item_emb, user_tile_item, item_blocks)
    items_for_tags = pick_blocks(item_emb, tag_tile_item, item_blocks)
    user_cols = lax.dynamic_slice_in_dim(user_emb, offset, BLK, 1)
    tag_cols = lax.dynamic_slice_in_dim(tag_emb, offset, BLK, 1)
    item_cols = lax.dynamic_slice_in_dim(item_emb, offset, BLK, 1)
    gram_part = jnp.einsum(
        "rj,rk->jk", user_cols, user_emb, precision=EXACT_PRECISION
    ) + jnp.einsum("rj,rk->jk", tag_cols, tag_emb, precision=EXACT_PRECISION)
    observed_part = item_terms(
        user_tiles, items_for_users, user_weight, offset, user_tile_item, item_blocks
    ) + item_terms(tag_tiles, items_for_tags, tag_weight, offset, tag_tile_item, item_blocks)
    gram_rows, observed = lax.psum((gram_part, observed_part), "ut")
    gram_square = lax.dynamic_slice_in_dim(gram_rows, offset, BLK, 1)
    item_right = (
        observed
        - UNSEEN_WEIGHT * jnp.einsum("ik,jk->ij", item_emb, gram_rows, precision=EXACT_PRECISION)
        - PENALTY * item_cols
    )

    def item_operator(direction):
        local_part = item_product(
            user_col_tiles, user_weight, direction, user_tile_item, item_blocks
        ) + item_product(tag_col_tiles, tag_weight, direction, tag_tile_item, item_blocks)
        return (
            lax.psum(local_part, "ut")
            + UNSEEN_WEIGHT
            * jnp.dot(
                direction,
                gram_square,
                precision=EXACT_PRECISION,
                preferred_element_type=jnp.float32,
            )
            + PENALTY * direction
        )

    item_block = item_cols + conjugate(item_right, item_operator)
    new_items = lax.dynamic_update_slice_in_dim(item_emb, item_block, offset, 1)
    new_for_users = pick_blocks(new_items, user_tile_item, item_blocks)
    new_for_tags = pick_blocks(new_items, tag_tile_item, item_blocks)
    user_item_cols = lax.dynamic_slice_in_dim(new_for_users, offset, BLK, 2)
    tag_item_cols = lax.dynamic_slice_in_dim(new_for_tags, offset, BLK, 2)
    gram_part_rows = jnp.einsum("ij,ik->jk", item_block, new_items, precision=EXACT_PRECISION)
    observed_rows = jnp.concatenate(
        [
            row_terms(user_tiles, new_for_users, user_weight, offset, user_tile_block, user_blocks),
            row_terms(tag_tiles, new_for_tags, tag_weight, offset, tag_tile_block, tag_blocks),
        ],
        axis=0,
    )
    all_rows = jnp.concatenate([user_emb, tag_emb], axis=0)
    row_cols = jnp.concatenate([user_cols, tag_cols], axis=0)

    def row_local(direction):
        return jnp.concatenate(
            [
                row_product(
                    user_item_cols,
                    user_weight,
                    direction[:user_total],
                    user_tile_block,
                    user_blocks,
                ),
                row_product(
                    tag_item_cols, tag_weight, direction[user_total:], tag_tile_block, tag_blocks
                ),
            ],
            axis=0,
        )

    item_gram, observed_sum = lax.psum((gram_part_rows, observed_rows), "it")
    item_square = lax.dynamic_slice_in_dim(item_gram, offset, BLK, 1)
    row_right = (
        observed_sum
        - UNSEEN_WEIGHT * jnp.einsum("rk,jk->rj", all_rows, item_gram, precision=EXACT_PRECISION)
        - PENALTY * row_cols
    )

    def row_operator(direction):
        return (
            lax.psum(row_local(direction), "it")
            + UNSEEN_WEIGHT
            * jnp.dot(
                direction,
                item_square,
                precision=EXACT_PRECISION,
                preferred_element_type=jnp.float32,
            )
            + PENALTY * direction
        )

    solution = row_cols + conjugate(row_right, row_operator)
    return (item_block, solution[:user_total], solution[user_total:])


BF16 = jnp.bfloat16
F32 = jnp.float32
MESH = pl.DeviceIdType.MESH


def halves(value):
    high = value.astype(BF16)
    return high, (value - high.astype(F32)).astype(BF16)


def dot_nt(left, right):
    return lax.dot_general(left, right, (((1,), (1,)), ((), ())), preferred_element_type=F32)


def dot_nn(left, right):
    return lax.dot_general(left, right, (((1,), (0,)), ((), ())), preferred_element_type=F32)


def stacked(value):
    return jnp.concatenate(halves(value), axis=0)


def paired(value):
    return jnp.concatenate(halves(value), axis=1)


def twice(value):
    both = stacked(value)
    return jnp.concatenate([both, both], axis=1)


def fold(total):
    rows = total.shape[0] // 2
    return total[:rows, :BLK] + total[:rows, BLK:] + total[rows:, :BLK] + total[rows:, BLK:]


def fold_rows(total):
    rows = total.shape[0] // 2
    return total[:rows] + total[rows:]


def solve(right_side, weight_ref, table_ref):
    chunks = weight_ref.shape[0]

    def step(_, carry):
        result, leftover, direction, norm_now = carry
        operand = twice(direction)
        total = None
        for j in range(chunks):
            inner = fold_rows(dot_nt(operand, table_ref[j]))
            term = dot_nn(stacked(weight_ref[j] * inner), table_ref[j])
            total = term if total is None else total + term
        applied = fold(total) + PENALTY * direction
        length = norm_now / (jnp.sum(direction * applied, axis=1, keepdims=True) + EPSILON)
        result = result + length * direction
        leftover = leftover - length * applied
        norm_next = jnp.sum(leftover * leftover, axis=1, keepdims=True)
        direction = leftover + norm_next / (norm_now + EPSILON) * direction
        return result, leftover, direction, norm_next

    norm = jnp.sum(right_side * right_side, axis=1, keepdims=True)
    start = (jnp.zeros_like(right_side), right_side, right_side, norm)
    return lax.fori_loop(0, CG_STEPS, step, start)[0]


def kernel(
    nu, ni, total_copies,
    ub_hbm, ui_hbm, tb_hbm, ti_hbm,
    user_hbm, tag_hbm, item_hbm, uc_hbm, tc_hbm,
    item_out, user_out, tag_out,
    ub_ref, ui_ref, tb_ref, ti_ref, user_ref, tag_ref, item_ref, uc_ref, tc_ref, local_sem,
    place, place_u, place_i, at, rat, ar, rar, wj, w2, hh, hl, e0, re0, est, part, rpart,
    at_own, a_own, ib, ib2, out, send_sem, recv_sem,
):
    k = lax.axis_index("ut")
    m = lax.axis_index("it")
    tile = uc_ref.shape[1]
    ut, tt = uc_ref.shape[0], tc_ref.shape[0]
    users, tags, items = user_ref.shape[0], tag_ref.shape[0], item_ref.shape[0]
    nub, ntb, nib = users // tile, tags // tile, items // tile
    nrb = nub + ntb
    rows = users + tags
    sub_i, sub_r = tile // nu, tile // ni
    share = rows // ni
    chips = ni // 2
    chip, core = m // 2, m % 2
    other = 1 - core
    sibling = 2 * chip + other

    def u_to(d):
        return (k + d) % nu

    def u_from(d):
        return (k + nu - d) % nu

    def i_to(d):
        return (m + d) % ni

    def i_from(d):
        return (m + ni - d) % ni

    def c_to(d):
        return (chip + d) % chips

    def c_from(d):
        return (chip + chips - d) % chips

    sent = []
    count = [0]

    def ticket():
        count[0] += 1
        return count[0] - 1

    def copy(number, source, target, device):
        return pltpu.make_async_remote_copy(
            src_ref=source, dst_ref=target, send_sem=send_sem.at[number],
            recv_sem=recv_sem.at[number], device_id=device, device_id_type=MESH,
        )

    def send(number, source, target, device):
        moving = copy(number, source, target, device)
        moving.start()
        sent.append(moving)

    def arrived(number, target):
        copy(number, target, target, (u_to(1), m)).wait_recv()

    barrier = pltpu.get_barrier_semaphore()
    for d in range(1, nu):
        pl.semaphore_signal(barrier, inc=1, device_id=(u_to(d), m), device_id_type=MESH)
    for d in range(1, ni):
        pl.semaphore_signal(barrier, inc=1, device_id=(k, i_to(d)), device_id_type=MESH)

    pairs = (
        (user_hbm.at[:, 0:BLK], wj.at[k, 0:users, :]), (tag_hbm.at[:, 0:BLK], wj.at[k, users:rows, :]),
        (ub_hbm, ub_ref), (ui_hbm, ui_ref), (tb_hbm, tb_ref), (ti_hbm, ti_ref),
        (uc_hbm, uc_ref), (tc_hbm, tc_ref), (item_hbm, item_ref), (user_hbm, user_ref), (tag_hbm, tag_ref),
    )
    loads = [pltpu.make_async_copy(a, b, local_sem.at[i]) for i, (a, b) in enumerate(pairs)]
    for load in loads:
        load.start()
    for load in loads[2:8]:
        load.wait()
    line = lax.broadcasted_iota(jnp.int32, place.shape, 0)
    spots = jnp.zeros(place.shape, jnp.int32)
    for t in range(ut):
        spots = jnp.where(line == t, ub_ref[t] * nib + ui_ref[t], spots)
    for t in range(tt):
        spots = jnp.where(line == ut + t, (nub + tb_ref[t]) * nib + ti_ref[t], spots)
    place[...] = spots
    for t in range(ut + tt):
        counts = CONFIDENCE * (uc_ref[t] if t < ut else tc_ref[t - ut]).astype(F32)
        ar[t] = counts
        at[t] = counts.T

    for load in loads[:2]:
        load.wait()
    pl.semaphore_wait(barrier, nu + ni - 2)

    def w_slice(kk, mm):
        return wj.at[kk, pl.ds(pl.multiple_of(mm * share, 8), share), :]

    def b_slice(kk, mm):
        return ib.at[mm, :, pl.ds(pl.multiple_of(kk * sub_i, 8), sub_i), :]

    far = sorted(range(1, nu), key=lambda d: min(d, nu - d))

    def tickets(first):
        z = {d: ticket() for d in range(1, nu)}
        p = {(d, e): ticket() for d in range(first, nu) for e in range(1, chips)}
        s = {(d, e): ticket() for d in range(first, nu) for e in range(chips)}
        return z, p, s

    def spread_along(piece, marks):
        for d in far:
            send(marks[0][d], piece(k, m), piece(k, m), (u_to(d), m))

    def spread_plane(piece, marks, d):
        held = piece(u_from(d), m)
        for e in range(1, chips):
            send(marks[1][d, e], held, held, (k, 2 * c_to(e) + core))
        send(marks[2][d, 0], held, held, (k, sibling))

    def spread_sibling(piece, marks, d):
        for e in range(1, chips):
            held = piece(u_from(d), 2 * c_from(e) + core)
            arrived(marks[1][d, e], held)
            send(marks[2][d, e], held, held, (k, sibling))

    def spread_finish(piece, marks, d):
        for e in range(chips):
            arrived(marks[2][d, e], piece(u_from(d), 2 * c_from(e) + other))

    w_marks = tickets(1)
    spread_along(w_slice, w_marks)
    at_marks = {d: (ticket(), ticket()) for d in range(1, nu)}

    def at_cut(kk):
        return at.at[:, pl.ds(pl.multiple_of(kk * sub_i, 8), sub_i), :]

    def r_cut(ref, mm):
        return ref.at[:, pl.ds(pl.multiple_of(mm * sub_r, 8), sub_r), :]

    for d in far:
        send(at_marks[d][0], at_cut(u_to(d)), rat.at[k], (u_to(d), m))
        send(at_marks[d][1], place, place_u.at[k], (u_to(d), m))
    ar_marks = {d: (ticket(), ticket()) for d in range(1, ni)}
    for d in range(1, ni):
        send(ar_marks[d][0], r_cut(ar, i_to(d)), rar.at[m], (k, i_to(d)))
        send(ar_marks[d][1], place, place_i.at[m], (k, i_to(d)))
    rat[k] = at[:, pl.ds(pl.multiple_of(k * sub_i, 8), sub_i), :]
    rar[m] = ar[:, pl.ds(pl.multiple_of(m * sub_r, 8), sub_r), :]
    place_u[k] = place[...]
    place_i[m] = place[...]

    def dense(spot_rows, tiles, block, piece):
        total = None
        for t in (range(ut) if block < nub else range(ut, ut + tt)):
            code = block * nib + piece
            term = jnp.where(spot_rows[t : t + 1, :] == code, tiles(t), 0.0)
            total = term if total is None else total + term
        return total

    for load in loads[8:]:
        load.wait()
    high, low = halves(item_ref[...])
    hh[...] = high
    hl[...] = low
    spot_rows = place[...]
    step = 2 if nub % 2 == 0 and ntb % 2 == 0 else 1

    def terms(first):
        block = user_ref[first * tile : (first + step) * tile, :] if first < nub else (
            tag_ref[(first - nub) * tile : (first - nub + step) * tile, :])
        rh, rl = halves(block)

        def product(cols):
            return (dot_nt(rh[:, cols], hh[:, cols]) + dot_nt(rh[:, cols], hl[:, cols])
                    + dot_nt(rl[:, cols], hh[:, cols]))

        rest = product(slice(BLK, None))
        mine = product(slice(0, BLK))
        counts = jnp.concatenate([
            jnp.concatenate([dense(spot_rows, lambda t: ar[t], b, p) for p in range(nib)], axis=1)
            for b in range(first, first + step)], axis=0)
        weight = counts + UNSEEN_WEIGHT
        begun = counts - weight * rest
        leftover = (begun - weight * mine).T
        eh, el = halves(leftover)
        span = slice(first * tile, (first + step) * tile)
        est[0:items, span] = eh
        est[items:, span] = el
        for b in range(step):
            e0[first + b] = begun[b * tile : (b + 1) * tile]

    firsts = list(range(0, nrb, step))
    for first in firsts[: len(firsts) // 2]:
        terms(first)
    for d in far:
        arrived(w_marks[0][d], w_slice(u_from(d), m))
        spread_plane(w_slice, w_marks, d)
    for first in firsts[len(firsts) // 2 :]:
        terms(first)
    w2[k] = paired(wj[k])
    summed = fold(dot_nn(est[...], w2[k]))
    for p in range(nib):
        part[p] = summed[p * tile : (p + 1) * tile]
    p_marks = {d: ticket() for d in range(1, nu)}
    for d in far:
        send(p_marks[d], at_like(part, u_to(d), sub_i), rpart.at[k], (u_to(d), m))
    rpart[k] = part[:, pl.ds(pl.multiple_of(k * sub_i, 8), sub_i), :]
    for d in far:
        spread_sibling(w_slice, w_marks, d)
    e_marks = {d: ticket() for d in range(1, ni)}
    for d in range(1, ni):
        send(e_marks[d], r_cut(e0, i_to(d)), re0.at[m], (k, i_to(d)))
    re0[m] = e0[:, pl.ds(pl.multiple_of(m * sub_r, 8), sub_r), :]

    for d in far:
        arrived(at_marks[d][0], rat.at[u_from(d)])
        arrived(at_marks[d][1], place_u.at[u_from(d)])

    def lay_items(kk, none):
        spot = place_u[kk]
        for p in range(nib):
            for b in range(nrb):
                at_own[kk, p * sub_i : (p + 1) * sub_i, b * tile : (b + 1) * tile] = (
                    dense(spot, lambda t: rat[kk, t], b, p) + UNSEEN_WEIGHT)
        return none

    lax.fori_loop(0, nu, lay_items, 0)
    for d in range(1, ni):
        arrived(ar_marks[d][0], rar.at[i_from(d)])
        arrived(ar_marks[d][1], place_i.at[i_from(d)])

    def lay_rows(mm, none):
        spot = place_i[mm]
        for b in range(nrb):
            for p in range(nib):
                a_own[mm, b * sub_r : (b + 1) * sub_r, p * tile : (p + 1) * tile] = (
                    dense(spot, lambda t: rar[mm, t], b, p) + UNSEEN_WEIGHT)
        return none

    lax.fori_loop(0, ni, lay_rows, 0)
    for d in far:
        spread_finish(w_slice, w_marks, d)
        source = u_from(d)
        w2[source] = paired(wj[source])
    for d in far:
        arrived(p_marks[d], rpart.at[u_from(d)])
    observed = rpart[0]
    for kk in range(1, nu):
        observed = observed + rpart[kk]
    own_items = jnp.concatenate([
        item_ref[pl.ds(pl.multiple_of(p * tile + k * sub_i, 8), sub_i), 0:BLK] for p in range(nib)], axis=0)
    right = observed.reshape(nib * sub_i, BLK) - PENALTY * own_items
    block = own_items + solve(right, at_own, w2)
    ib[m, :, pl.ds(pl.multiple_of(k * sub_i, 8), sub_i), :] = block.reshape(nib, sub_i, BLK)

    own_rows = jnp.concatenate(
        [user_ref[pl.ds(pl.multiple_of(b * tile + m * sub_r, 8), sub_r), 0:BLK] for b in range(nub)]
        + [tag_ref[pl.ds(pl.multiple_of(b * tile + m * sub_r, 8), sub_r), 0:BLK] for b in range(ntb)], axis=0)
    operand = twice(own_rows)

    b_marks = tickets(0)
    spread_along(b_slice, b_marks)
    spread_plane(b_slice, b_marks, 0)
    for d in far:
        arrived(b_marks[0][d], b_slice(u_from(d), m))
        spread_plane(b_slice, b_marks, d)
    for d in range(1, ni):
        arrived(e_marks[d], re0.at[i_from(d)])

    def gather(mm, total):
        table = paired(ib[mm].reshape(items, BLK))
        ib2[mm] = table
        inner = fold_rows(dot_nt(operand, table))
        leftover = re0[mm].reshape(share, items) - a_own[mm] * inner
        term = dot_nn(stacked(leftover), table)
        return term if total is None else total + term

    spread_sibling(b_slice, b_marks, 0)
    total = gather(m, None)
    for d in far:
        spread_sibling(b_slice, b_marks, d)
    for e in range(1, chips):
        total = gather(2 * c_from(e) + core, total)
    for e in range(chips):
        for d in [0] + far:
            arrived(b_marks[2][d, e], b_slice(u_from(d), 2 * c_from(e) + other))
        total = gather(2 * c_from(e) + other, total)
    right = fold(total) - PENALTY * own_rows
    final = own_rows + solve(right, a_own, ib2)
    out[:, pl.ds(pl.multiple_of(m * sub_r, 8), sub_r), :] = final.reshape(nrb, sub_r, BLK)
    mine = r_cut(out, m)
    o_marks = {e: ticket() for e in range(1, chips)}
    x_marks = {e: ticket() for e in range(chips)}
    for e in range(1, chips):
        send(o_marks[e], mine, mine, (k, 2 * c_to(e) + core))
    send(x_marks[0], mine, mine, (k, sibling))

    def leave(i, source, target):
        moving = pltpu.make_async_copy(source, target, local_sem.at[i])
        moving.start()
        return moving

    leaving = [leave(p, ib.at[m, p], item_out.at[p * tile : (p + 1) * tile, :]) for p in range(nib)]
    for e in range(1, chips):
        held = r_cut(out, 2 * c_from(e) + core)
        arrived(o_marks[e], held)
        send(x_marks[e], held, held, (k, sibling))
    for e in range(chips):
        arrived(x_marks[e], r_cut(out, 2 * c_from(e) + other))
    for b in range(nub):
        leaving.append(leave(nib + b, out.at[b], user_out.at[b * tile : (b + 1) * tile, :]))
    for b in range(ntb):
        leaving.append(leave(nib + nub + b, out.at[nub + b], tag_out.at[b * tile : (b + 1) * tile, :]))
    for moving in leaving:
        moving.wait()
    for moving in sent:
        moving.wait_send()
    if count[0] != total_copies:
        raise ValueError(count[0])


def at_like(ref, index, size):
    return ref.at[:, pl.ds(pl.multiple_of(index * size, 8), size), :]


def fused(
    nu, ni, user_emb, tag_emb, item_emb, user_tile_block, user_tile_item, user_tile_counts,
    tag_tile_block, tag_tile_item, tag_tile_counts,
):
    tile = user_tile_counts.shape[1]
    tiles = user_tile_counts.shape[0] + tag_tile_counts.shape[0]
    users, tags, (items, rank) = user_emb.shape[0], tag_emb.shape[0], item_emb.shape
    rows = users + tags
    nrb, nib = rows // tile, items // tile
    sub_i, sub_r, share, chips = tile // nu, tile // ni, rows // ni, ni // 2
    lines = -(-tiles // 8) * 8
    copies = (
        (nu - 1) + (nu - 1) * (2 * chips - 1) + (nu - 1) + nu * (2 * chips - 1)
        + 3 * (nu - 1) + 3 * (ni - 1) + 2 * chips - 1
    )
    hbm = pl.BlockSpec(memory_space=pltpu.HBM)
    return pl.pallas_call(
        functools.partial(kernel, nu, ni, copies),
        out_shape=(
            jax.ShapeDtypeStruct((items, BLK), F32),
            jax.ShapeDtypeStruct((users, BLK), F32),
            jax.ShapeDtypeStruct((tags, BLK), F32),
        ),
        in_specs=[hbm] * 9,
        out_specs=(hbm, hbm, hbm),
        scratch_shapes=[
            pltpu.SMEM(user_tile_block.shape, jnp.int32),
            pltpu.SMEM(user_tile_item.shape, jnp.int32),
            pltpu.SMEM(tag_tile_block.shape, jnp.int32),
            pltpu.SMEM(tag_tile_item.shape, jnp.int32),
            pltpu.VMEM(user_emb.shape, F32),
            pltpu.VMEM(tag_emb.shape, F32),
            pltpu.VMEM(item_emb.shape, F32),
            pltpu.VMEM(user_tile_counts.shape, jnp.int32),
            pltpu.VMEM(tag_tile_counts.shape, jnp.int32),
            pltpu.SemaphoreType.DMA((max(11, nib + nrb),)),
            pltpu.VMEM((lines, 128), jnp.int32),
            pltpu.VMEM((nu, lines, 128), jnp.int32),
            pltpu.VMEM((ni, lines, 128), jnp.int32),
            pltpu.VMEM((tiles, tile, tile), F32),
            pltpu.VMEM((nu, tiles, sub_i, tile), F32),
            pltpu.VMEM((tiles, tile, tile), F32),
            pltpu.VMEM((ni, tiles, sub_r, tile), F32),
            pltpu.VMEM((nu, rows, BLK), F32),
            pltpu.VMEM((nu, rows, 2 * BLK), BF16),
            pltpu.VMEM((items, rank), BF16),
            pltpu.VMEM((items, rank), BF16),
            pltpu.VMEM((nrb, tile, items), F32),
            pltpu.VMEM((ni, nrb, sub_r, items), F32),
            pltpu.VMEM((2 * items, rows), BF16),
            pltpu.VMEM((nib, tile, BLK), F32),
            pltpu.VMEM((nu, nib, sub_i, BLK), F32),
            pltpu.VMEM((nu, nib * sub_i, rows), F32),
            pltpu.VMEM((ni, share, items), F32),
            pltpu.VMEM((ni, nib, tile, BLK), F32),
            pltpu.VMEM((ni, items, 2 * BLK), BF16),
            pltpu.VMEM((nrb, tile, BLK), F32),
            pltpu.SemaphoreType.DMA((copies,)),
            pltpu.SemaphoreType.DMA((copies,)),
        ],
        compiler_params=pltpu.CompilerParams(
            collective_id=0, has_side_effects=True, vmem_limit_bytes=64 * 1024 * 1024
        ),
    )(
        user_tile_block, user_tile_item, tag_tile_block, tag_tile_item,
        user_emb, tag_emb, item_emb, user_tile_counts, tag_tile_counts,
    )


def serves(nu, ni, tile):
    return nu > 1 and ni > 2 and ni % 2 == 0 and tile % (nu * 8) == 0 and tile % (ni * 16) == 0


def solution(mesh):
    placed = (
        P("ut", None),
        P("ut", None),
        P("it", None),
        P(("ut", "it")),
        P(("ut", "it")),
        P(("ut", "it"), None, None),
        P(("ut", "it")),
        P(("ut", "it")),
        P(("ut", "it"), None, None),
    )
    nu, ni = mesh.shape["ut"], mesh.shape["it"]

    def run(*arrays):
        if serves(nu, ni, arrays[5].shape[1]):
            return fused(nu, ni, *arrays)
        return local(*arrays)

    return jax.shard_map(
        run,
        mesh=mesh,
        in_specs=placed,
        out_specs=(P("it", None), P("ut", None), P("ut", None)),
        check_vma=False,
    )
```
